32 devices in a mesh: dp: 4 (over z), pipe: 4 (over y, x), tensor: 2 (over core).
Axes of the slice: x: 2, y: 2, z: 4, core: 2. Of those that a mesh axis runs over, the one named last changes fastest.
Arguments:
- embeds: bfloat16 [16, 64, 4096], P('dp', 'tensor'), parts along dimension 0, may hold values from -6 to 6
- labels: int32 [16, 64], P('dp'), parts along dimension 0, may hold values from 0 to 6143
- norm_gain: float32 [4, 4096], P('pipe'), may hold values from 0.5 to 1.5
- w_query: bfloat16 [4, 4096, 2048], P('pipe', None, 'tensor'), may hold values from -0.09375 to 0.09375
- w_key: bfloat16 [4, 4096, 1024], P('pipe', None, 'tensor'), may hold values from -0.09375 to 0.09375
- w_value: bfloat16 [4, 4096, 1024], P('pipe', None, 'tensor'), may hold values from -0.09375 to 0.09375
- w_out: bfloat16 [4, 2048, 4096], P('pipe', 'tensor'), may hold values from -0.125 to 0.125
- final_gain: float32 [4096], replicated, may hold values from 0.5 to 1.5
- head_weight: bfloat16 [4096, 6144], P(None, ('pipe', 'tensor')), may hold values from -16 to 16
Outputs:
- token_loss: float32 [16, 64], P('dp', ('pipe', 'tensor')), parts along dimension 0
- scores: float32 [16], P('dp'), parts along dimension 0
The draws below stay inside these ranges and needn't reach their ends.
There are 4 independent parts, one for each index of `dp`. The reference program is written for one: setup_inputs(seed, part) draws one part's arguments, and reference() takes and returns one part's arrays. A program takes and returns all parts, laid end to end along the dimension named above; an argument that names none is the same for every part. Nothing has to cross between parts.
All inputs are finite; a program needn't handle non-finite values.
Results may differ from the reference program's by a relative error of at most 0.014.
Values may be sent and summed in bfloat16 or wider, within the bound.
A program may use at most 128 MiB of HBM per device.

```python
import math
import jax
import jax.numpy as jnp
import numpy as np
from jax import lax

D = 4096
HD = 128
KVH = 8
QH = 16
MICRO = 4
SEQ = 64
LAYERS = 4
VOCAB = 6144
N_TENSOR = 2


def draw_head_weight(key, part):
    key_base, key_scale = jax.random.split(jax.random.fold_in(key, 17))
    base = jax.random.truncated_normal(key_base, -3.0, 3.0, (D, VOCAB), jnp.float32)
    column_scale = 3.0 + 0.0 * jax.random.uniform(key_scale, (1, VOCAB), jnp.float32)
    return (base * column_scale / math.sqrt(D)).astype(jnp.bfloat16)


def touch_ends(values, rng, smallest, top_value):
    extent = values.shape
    spot = [jax.random.randint(jax.random.fold_in(rng, axis), (), 0, extent[axis]) for axis in range(len(extent))]
    values = values.at[tuple(spot)].set(smallest)
    longest = extent.index(max(extent))
    spot[longest] = (spot[longest] + 1) % extent[longest]
    return values.at[tuple(spot)].set(top_value)


def level_of(own_key, dims, cuts, smallest, high):
    factor_of, own = 1.0, jax.random.fold_in(own_key, 6)
    for position, parts in cuts:
        heights = jnp.exp(jax.random.uniform(jax.random.fold_in(own, position), (parts,), jnp.float32, smallest / len(cuts), high / len(cuts)))
        factor_of = factor_of * jnp.repeat(heights, dims[position] // parts).reshape([-1 if axis == position else 1 for axis in range(len(dims))])
    return factor_of


def rank_table(number_of, slope):
    weights = [(1 << 20) // math.isqrt(standing ** slope) + 1 for standing in range(1, number_of + 1)]
    width = 1 + sum(weights) // (1 << 30)
    return np.cumsum(np.array([max(1, weight // width) for weight in weights]))


def ranked(own_key, shape, number_of, slope):
    listing = rank_table(number_of, slope)
    ticket = jax.random.randint(jax.random.fold_in(own_key, 1), shape, 0, int(listing[number_of - 1]))
    standing = jnp.searchsorted(jnp.asarray(listing, jnp.int32), ticket, side="right")
    return jax.random.permutation(jax.random.fold_in(own_key, 2), number_of)[standing].astype(jnp.int32)


def bell_draw(rng, dims, deviation, bound, cuts=(), kind=jnp.bfloat16):
    entries = jax.random.normal(rng, dims, jnp.float32) * deviation
    if len(cuts) > 0:
        entries = level_of(rng, dims, cuts, -0.22, 0.18) * entries
    return jnp.clip(entries, min=-bound, max=bound).astype(kind)


def setup_inputs(seed: int = 0, part: int = 0) -> dict:
    streams_of = jax.random.split(jax.random.key(seed), 10)
    part_splits = jax.random.split(jax.random.fold_in(streams_of[9], part), 10)
    return {
        "embeds": bell_draw(part_splits[0], (MICRO, SEQ, D), 1.0, 6.0, ((1, 2),)),
        "labels": touch_ends(ranked(part_splits[1], (MICRO, SEQ), VOCAB, 1), jax.random.fold_in(part_splits[1], 3), 0, VOCAB - 1).astype(jnp.int32),
        "norm_gain": jnp.clip(1.0 + 0.1 * jax.random.normal(streams_of[2], (LAYERS, D), jnp.float32), 0.5, 1.5),
        "w_query": bell_draw(streams_of[3], (LAYERS, D, QH * HD), D ** -0.5, 0.09375, ((0, 4), (2, 2))),
        "w_key": bell_draw(streams_of[4], (LAYERS, D, KVH * HD), D ** -0.5, 0.09375, ((0, 4), (2, 2))),
        "w_value": bell_draw(streams_of[5], (LAYERS, D, KVH * HD), D ** -0.5, 0.09375, ((0, 4), (2, 2))),
        "w_out": bell_draw(streams_of[6], (LAYERS, QH * HD, D), (QH * HD) ** -0.5, 0.125, ((0, 4), (1, 2))),
        "final_gain": jnp.clip(1.0 + 0.1 * jax.random.normal(streams_of[7], (D,), jnp.float32), 0.5, 1.5),
        "head_weight": draw_head_weight(jax.random.fold_in(streams_of[9], 71), part),
    }


EPSILON = 1e-05
ROPE_BASE = 500000.0

def normalize(states, gain_vec):
    values = states.astype(jnp.float32)
    return values * lax.rsqrt(lax.optimization_barrier(jnp.mean(values * values, axis=-1, keepdims=True)) + EPSILON) * gain_vec

def rotate(tensor, positions):
    half_dim = tensor.shape[-1] // 2
    index = jnp.arange(half_dim, dtype=jnp.float32)
    inverse = ROPE_BASE ** (-2.0 * index / tensor.shape[-1])
    angles = positions[:, None] * inverse[None, :]
    cosine = jnp.cos(angles)[:, None, :]
    sine = jnp.sin(angles)[:, None, :]
    first_half = tensor[..., :half_dim]
    second_half = tensor[..., half_dim:]
    return jnp.concatenate([first_half * cosine - second_half * sine, second_half * cosine + first_half * sine], axis=-1)

def project(normed, layer_query, layer_key, layer_value):
    n_rows = normed.shape[0]
    positions = jnp.arange(n_rows).astype(jnp.float32)
    query = jnp.dot(normed, layer_query, preferred_element_type=jnp.float32)
    query = rotate(query.reshape(n_rows, -1, HD), positions).reshape(n_rows, -1)
    keys = jnp.dot(normed, layer_key, preferred_element_type=jnp.float32)
    keys = rotate(keys.reshape(n_rows, -1, HD), positions).reshape(n_rows, -1)
    values = jnp.dot(normed, layer_value, preferred_element_type=jnp.float32)
    return jnp.concatenate([query, keys, values], axis=1)

def attend(projected, heads_q, heads_kv):
    n_rows = projected.shape[0]
    q_width = heads_q * HD
    k_width = heads_kv * HD
    query = projected[:, :q_width].reshape(n_rows, heads_kv, heads_q // heads_kv, HD).astype(jnp.float32)
    keys = projected[:, q_width:q_width + k_width].reshape(n_rows, heads_kv, HD).astype(jnp.float32)
    values = projected[:, q_width + k_width:].reshape(n_rows, heads_kv, HD).astype(jnp.float32)
    logits = jnp.einsum('skgd,tkd->kgst', query, keys) / math.sqrt(HD)
    causal = jnp.arange(n_rows)[:, None] >= jnp.arange(n_rows)[None, :]
    weights_attn = jax.nn.softmax(jnp.where(causal, logits, -1e+30), axis=-1).astype(jnp.bfloat16)
    context = jnp.einsum('kgst,tkd->skgd', weights_attn.astype(jnp.float32), values)
    return context.astype(jnp.bfloat16).reshape(n_rows, q_width)

def reference(embeds, labels, norm_gain, w_query, w_key, w_value, w_out, final_gain, head_weight):
    group_width = QH * HD // N_TENSOR
    states = [embeds[seq_index] for seq_index in range(MICRO)]
    for layer in range(LAYERS):
        out_grouped = w_out[layer].reshape(N_TENSOR, group_width, D).astype(jnp.float32)
        updated = []
        for state in states:
            normed = normalize(state, norm_gain[layer]).astype(jnp.bfloat16)
            projected = project(normed, w_query[layer], w_key[layer], w_value[layer]).astype(jnp.bfloat16)
            context = attend(projected, QH, KVH)
            grouped = context.reshape(SEQ, N_TENSOR, group_width).astype(jnp.float32)
            partial_sums = jnp.einsum('snc,ncd->nsd', grouped, out_grouped)
            rounded = lax.optimization_barrier(partial_sums.astype(jnp.bfloat16))
            block = lax.optimization_barrier(jnp.sum(rounded.astype(jnp.float32), axis=0))
            updated.append((state.astype(jnp.float32) + block).astype(jnp.bfloat16))
        states = updated
    hidden = normalize(jnp.stack(states), final_gain).astype(jnp.bfloat16)
    flat_rows = hidden.reshape(MICRO * SEQ, D)
    logits = jnp.dot(flat_rows, head_weight, preferred_element_type=jnp.float32)
    peak_row = lax.optimization_barrier(jnp.max(logits, axis=-1, keepdims=True))
    log_norm = peak_row[:, 0] + jnp.log(lax.optimization_barrier(jnp.sum(jnp.exp(logits - peak_row), axis=-1)))
    flat_labels = labels.reshape(-1).astype(jnp.int32)
    target = jnp.take_along_axis(logits, flat_labels[:, None], axis=1)[:, 0]
    token_loss = (log_norm - target).reshape(MICRO, SEQ)
    onehot = flat_labels[:, None] == jnp.arange(VOCAB, dtype=jnp.int32)[None, :]
    errors = (jnp.exp(logits - log_norm[:, None]) - onehot.astype(jnp.float32)).astype(jnp.bfloat16)
    errors = errors.reshape(MICRO, SEQ, VOCAB).astype(jnp.float32)
    hidden_f = hidden.astype(jnp.float32)
    gram_err = jnp.einsum('bsv,btv->bst', errors, errors)
    gram_hid = jnp.einsum('bsd,btd->bst', hidden_f, hidden_f)
    totals = lax.optimization_barrier(jnp.sum(gram_err * gram_hid, axis=(1, 2)))
    scores = jnp.sqrt(totals) / SEQ
    return (token_loss, scores)
```

```python
import functools
import math

import jax
import jax.numpy as jnp
import numpy as np
from jax import lax
from jax.experimental import pallas as pl
from jax.experimental.pallas import tpu as pltpu
from jax.sharding import PartitionSpec as P

HD = 128
EPSILON = 1e-05
ROPE_BASE = 500000.0
LANES = 128
MESH = pl.DeviceIdType.MESH
NEG = -1e30


def round_up(value, step):
    return (value + step - 1) // step * step


def rotary_tables(seq_len):
    half = HD // 2
    inverse = (ROPE_BASE ** (-2.0 * np.arange(half, dtype=np.float64) / HD)).astype(np.float32)
    angles = (np.arange(seq_len, dtype=np.float32)[:, None] * inverse[None, :]).astype(np.float64)
    cosine, sine = np.cos(angles), np.sin(angles)
    cos_full = np.concatenate([cosine, cosine], axis=1)
    sin_full = np.concatenate([-sine, sine], axis=1)
    cos_table = np.stack([cos_full, np.ones_like(cos_full)]).astype(np.float32)
    sin_table = np.stack([sin_full, np.zeros_like(sin_full)]).astype(np.float32)
    return cos_table, sin_table


def relay_kernel(
    dims,
    embeds_ref, labels_ref, gain_ref, w_query_ref, w_key_ref, w_value_ref, w_out_ref,
    final_gain_ref, head_ref, cos_ref, sin_ref,
    loss_ref, score_ref,
    wqkv, wout, whead, st_in, gat, flat, qkv, ctx, part, rs, outst, hid, logits, ghid,
    labcol, slab, stats, tots,
    w_sem, wo_sem, wh_sem, e_sem,
    in_send, in_recv, g_send, g_recv, r_send, r_recv,
    h_send, h_recv, s_send, s_recv, t_send, t_recv, u_send, u_recv,
):
    n_pipe, n_tensor, micro, rows, width, heads_q, heads_kv, vocab_dev = dims
    group = n_pipe * n_tensor
    seq_len = rows * n_tensor
    kv_width = heads_kv * HD
    per_kv = heads_q // heads_kv
    n_tiles = per_kv + 2
    n_out, _, out_width = wout.shape
    last = n_pipe - 1
    half = width // 2
    p = lax.axis_index("pipe")
    t = lax.axis_index("tensor")
    slot = p * n_tensor + t
    near = [n_pipe - 2, n_pipe - 3] if n_pipe >= 3 else list(range(last))
    far = [q for q in range(last) if q not in near]

    def w_copy(i):
        if i < per_kv:
            src = w_query_ref.at[0, :, pl.ds(i * kv_width, kv_width)]
        else:
            src = (w_key_ref if i == per_kv else w_value_ref).at[0]
        return pltpu.make_async_copy(src, wqkv.at[i], w_sem.at[i])

    def wo_copy(n):
        return pltpu.make_async_copy(
            w_out_ref.at[0, :, pl.ds(n * out_width, out_width)], wout.at[n], wo_sem.at[n]
        )

    def e_copy(m, n):
        return pltpu.make_async_copy(
            embeds_ref.at[m, :, pl.ds(n * out_width, out_width)], st_in.at[m, n], e_sem.at[m, n]
        )

    head_copy = pltpu.make_async_copy(head_ref, whead, wh_sem)

    @pl.when(p == 0)
    def _():
        for m in range(micro):
            for n in range(n_out):
                e_copy(m, n).start()

    for i in range(n_tiles):
        w_copy(i).start()
    for n in range(n_out):
        wo_copy(n).start()
    head_copy.start()

    def ring(j):
        peer = lax.rem(slot + j, group)
        return peer, {"pipe": peer // n_tensor, "tensor": lax.rem(peer, n_tensor)}

    barrier = pltpu.get_barrier_semaphore()
    for j in range(1, group):
        pl.semaphore_signal(barrier, inc=1, device_id=ring(j)[1], device_id_type=MESH)
    pl.semaphore_wait(barrier, group - 1)

    @pl.when(p == 0)
    def _():
        for m in range(micro):
            for n in range(n_out):
                e_copy(m, n).wait()

    def remote(src, dst, send, recv, device):
        return pltpu.make_async_remote_copy(
            src_ref=src, dst_ref=dst, send_sem=send, recv_sem=recv,
            device_id=device, device_id_type=MESH,
        )

    def mate(j):
        return lax.rem(t + j, n_tensor)

    def in_copy(m, n):
        return remote(outst.at[m, n], st_in.at[m, n], in_send.at[m, n], in_recv.at[m, n],
                      {"pipe": lax.rem(p + 1, n_pipe)})

    def g_copy(m, j):
        return remote(gat.at[m, t], gat.at[m, t], g_send.at[m, j], g_recv.at[m, t],
                      {"tensor": mate(j)})

    def g_arrival(m, j):
        who = mate(j)
        return remote(gat.at[m, who], gat.at[m, who], g_send.at[m, j], g_recv.at[m, who],
                      {"tensor": who})

    def r_copy(m, n, j):
        who = mate(j)
        return remote(part.at[m, n, who], rs.at[m, n, t], r_send.at[m, n, j],
                      r_recv.at[m, n, t], {"tensor": who})

    def r_arrival(m, n, j):
        who = mate(j)
        return remote(part.at[m, n, who], rs.at[m, n, who], r_send.at[m, n, j],
                      r_recv.at[m, n, who], {"tensor": who})

    def h_copy(m, h, k, to):
        piece = hid.at[m, t, :, pl.ds(h * half, half)]
        return remote(piece, piece, h_send.at[m, h, k], h_recv.at[m, h], {"pipe": to})

    def s_copy(m, j):
        return remote(hid.at[m, t], hid.at[m, t], s_send.at[m, j], s_recv.at[m, t],
                      {"tensor": mate(j)})

    def s_arrival(m, j):
        who = mate(j)
        return remote(hid.at[m, who], hid.at[m, who], s_send.at[m, j], s_recv.at[m, who],
                      {"tensor": who})

    def scaled(squares):
        return lax.rsqrt(squares * (1.0 / width) + EPSILON)

    row_at = lax.broadcasted_iota(jnp.int32, (per_kv * seq_len, seq_len), 0)
    key_at = lax.broadcasted_iota(jnp.int32, (per_kv * seq_len, seq_len), 1)
    causal = lax.rem(row_at, seq_len) >= key_at

    def layer(m, carry):
        @pl.when(p > 0)
        def _():
            for n in range(n_out):
                in_copy(m, n).wait_recv()

        squares = jnp.zeros((rows, 1), jnp.float32)
        for n in range(n_out):
            tile = st_in[m, n].astype(jnp.float32)
            squares += jnp.sum(tile * tile, axis=-1, keepdims=True)
        factor = scaled(squares)
        for n in range(n_out):
            cols = pl.ds(n * out_width, out_width)
            normed = st_in[m, n].astype(jnp.float32) * factor * gain_ref[:, cols]
            gat[m, t, :, cols] = normed.astype(jnp.bfloat16)
        for j in range(1, n_tensor):
            g_copy(m, j).start()
        for j in range(1, n_tensor):
            g_arrival(m, j).wait_recv()
        if rows % 16:
            flat[...] = gat[m].astype(jnp.float32).reshape(seq_len, width).astype(jnp.bfloat16)

        @pl.when(m == 0)
        def _():
            for i in range(n_tiles):
                w_copy(i).wait()

        def project(i, c):
            lhs = flat[...] if rows % 16 else gat[m].reshape(seq_len, width)
            product = jnp.dot(lhs, wqkv[i], preferred_element_type=jnp.float32)
            which = jnp.where(i == n_tiles - 1, 1, 0)
            cosine, sine = cos_ref[which], sin_ref[which]
            for h in range(heads_kv):
                one = product[:, h * HD : (h + 1) * HD]
                turned = one * cosine + pltpu.roll(one, HD // 2, 1) * sine
                qkv[i, :, h * HD : (h + 1) * HD] = turned.astype(jnp.bfloat16)
            return c

        lax.fori_loop(0, n_tiles, project, 0)

        for h in range(heads_kv):
            queries = []
            for g in range(per_kv):
                head = h * per_kv + g
                at = head % heads_kv * HD
                queries.append(qkv[head // heads_kv, :, at : at + HD])
            query = jnp.concatenate(queries, axis=0) if per_kv > 1 else queries[0]
            key = qkv[per_kv, :, h * HD : (h + 1) * HD]
            value = qkv[per_kv + 1, :, h * HD : (h + 1) * HD]
            scores = lax.dot_general(
                query, key, (((1,), (1,)), ((), ())), preferred_element_type=jnp.float32
            ) * (1.0 / math.sqrt(HD))
            scores = jnp.where(causal, scores, NEG)
            shifted = jnp.exp(scores - jnp.max(scores, axis=-1, keepdims=True))
            probs = (shifted / jnp.sum(shifted, axis=-1, keepdims=True)).astype(jnp.bfloat16)
            context = jnp.dot(probs, value, preferred_element_type=jnp.float32)
            for g in range(per_kv):
                at = (h * per_kv + g) * HD
                ctx[:, at : at + HD] = context[g * seq_len : (g + 1) * seq_len].astype(jnp.bfloat16)

        @pl.when(m == 0)
        def _():
            for n in range(n_out):
                wo_copy(n).wait()

        def output(n, c):
            product = jnp.dot(ctx[...], wout[n], preferred_element_type=jnp.float32)
            part[m, n] = product.reshape(n_tensor, rows, out_width).astype(jnp.bfloat16)
            for j in range(1, n_tensor):
                r_copy(m, n, j).start()
            return c

        lax.fori_loop(0, n_out, output, 0)

        def combine(n, total):
            block = part[m, n, t].astype(jnp.float32)
            for j in range(1, n_tensor):
                r_arrival(m, n, j).wait_recv()
                block += rs[m, n, mate(j)].astype(jnp.float32)
            state = (st_in[m, n].astype(jnp.float32) + block).astype(jnp.bfloat16)
            outst[m, n] = state

            @pl.when(p < last)
            def _():
                in_copy(m, n).start()

            wide = state.astype(jnp.float32)
            return total + jnp.sum(wide * wide, axis=-1, keepdims=True)

        total = lax.fori_loop(0, n_out, combine, jnp.zeros((rows, 1), jnp.float32))

        @pl.when(p == last)
        def _():
            last_factor = scaled(total)
            for n in range(n_out):
                cols = pl.ds(n * out_width, out_width)
                final = outst[m, n].astype(jnp.float32) * last_factor * final_gain_ref[:, cols]
                hid[m, t, :, cols] = final.astype(jnp.bfloat16)
            for step in range(2):
                for k, to in enumerate(near):
                    h_copy(m, (k + 1 + step) % 2, k, to).start()

        return carry

    lax.fori_loop(0, micro, layer, 0)

    pad = jnp.zeros((LANES - micro, seq_len), jnp.float32)
    labcol[...] = jnp.concatenate([labels_ref[...].astype(jnp.float32), pad], axis=0).T
    slab[...] = jnp.zeros_like(slab)
    lane = lax.broadcasted_iota(jnp.int32, (seq_len, LANES), 1)
    entry = (lax.broadcasted_iota(jnp.int32, (seq_len, vocab_dev), 1) + slot * vocab_dev).astype(
        jnp.float32
    )

    def onehot_of(m):
        own = jnp.sum(jnp.where(lane == m, labcol[...], 0.0), axis=-1, keepdims=True)
        return entry == own

    head_copy.wait()

    def head(m, carry):
        if len(near) == 2 and far:
            for k in range(2):
                first = (k + 1) % 2

                @pl.when(p == near[k])
                def _():
                    h_copy(m, first, 0, 0).wait_recv()
                    for f, to in enumerate(far):
                        h_copy(m, first, f, to).start()
                    h_copy(m, 1 - first, 0, 0).wait_recv()

            @pl.when(p < near[1])
            def _():
                for h in range(2):
                    h_copy(m, h, 0, last).wait_recv()
        else:
            @pl.when(p < last)
            def _():
                for h in range(2):
                    h_copy(m, h, 0, last).wait_recv()

        for j in range(1, n_tensor):
            s_copy(m, j).start()
        for j in range(1, n_tensor):
            s_arrival(m, j).wait_recv()
        if rows % 16:
            flat[...] = hid[m].astype(jnp.float32).reshape(seq_len, width).astype(jnp.bfloat16)
            lhs = flat[...]
        else:
            lhs = hid[m].reshape(seq_len, width)
        local = jnp.dot(lhs, whead[...], preferred_element_type=jnp.float32)
        logits[m] = local
        peak = jnp.max(local, axis=-1, keepdims=True)
        mass = jnp.sum(jnp.exp(local - peak), axis=-1, keepdims=True)
        target = jnp.sum(jnp.where(onehot_of(m), local, 0.0), axis=-1, keepdims=True)
        slab[...] = jnp.where(
            lane == m,
            peak,
            jnp.where(lane == micro + m, mass, jnp.where(lane == 2 * micro + m, target, slab[...])),
        )
        ghid[m] = lax.dot_general(
            lhs, lhs, (((1,), (1,)), ((), ())), preferred_element_type=jnp.float32
        )
        return carry

    lax.fori_loop(0, micro, head, 0)

    n_stats = stats.shape[1]
    stats[slot] = slab[...].T[:n_stats]

    def exchange(buffer, send, recv):
        def copy(j):
            peer, device = ring(j)
            return remote(buffer.at[slot], buffer.at[slot], send.at[j], recv.at[slot], device)

        def arrival(j):
            peer, device = ring(j)
            return remote(buffer.at[peer], buffer.at[peer], send.at[j], recv.at[peer], device)

        for j in range(1, group):
            copy(j).start()
        for j in range(1, group):
            arrival(j).wait_recv()
        return copy

    stats_copy = exchange(stats, t_send, t_recv)
    peaks = stats[:, :micro, :]
    peak_row = jnp.max(peaks, axis=0)
    masses = jnp.exp(peaks - peak_row[None]) * stats[:, micro : 2 * micro, :]
    log_norm = peak_row + jnp.log(jnp.sum(masses, axis=0))
    loss_ref[...] = log_norm - jnp.sum(stats[:, 2 * micro : 3 * micro, :], axis=0)
    labels_t = labcol[...]
    norm_t = jnp.concatenate([log_norm, pad], axis=0).T

    tot_rows = tots.shape[1]
    row_id = lax.broadcasted_iota(jnp.int32, (tot_rows, seq_len), 0)
    sums = jnp.zeros((tot_rows, seq_len), jnp.float32)
    for m in range(micro):
        onehot = (entry == labels_t[:, m : m + 1]).astype(jnp.float32)
        errors = (jnp.exp(logits[m] - norm_t[:, m : m + 1]) - onehot).astype(jnp.bfloat16)
        gram = lax.dot_general(
            errors, errors, (((1,), (1,)), ((), ())), preferred_element_type=jnp.float32
        )
        sums = jnp.where(row_id == m, jnp.sum(gram * ghid[m], axis=0, keepdims=True), sums)
    tots[slot] = sums
    tots_copy = exchange(tots, u_send, u_recv)
    total = jnp.sum(jnp.sum(tots[...], axis=0), axis=-1, keepdims=True)
    score_ref[...] = jnp.broadcast_to(jnp.sqrt(total) / seq_len, score_ref.shape)

    def drain(m, carry):
        for j in range(1, n_tensor):
            g_copy(m, j).wait_send()
            s_copy(m, j).wait_send()
            for n in range(n_out):
                r_copy(m, n, j).wait_send()

        @pl.when(p < last)
        def _():
            for n in range(n_out):
                in_copy(m, n).wait_send()

        @pl.when(p == last)
        def _():
            for h in range(2):
                for k, to in enumerate(near):
                    h_copy(m, h, k, to).wait_send()

        if len(near) == 2 and far:
            for k in range(2):
                first = (k + 1) % 2

                @pl.when(p == near[k])
                def _():
                    for f, to in enumerate(far):
                        h_copy(m, first, f, to).wait_send()

        return carry

    lax.fori_loop(0, micro, drain, 0)
    for j in range(1, group):
        stats_copy(j).wait_send()
        tots_copy(j).wait_send()


def per_device(embeds, labels, norm_gain, w_query, w_key, w_value, w_out, final_gain, head_weight):
    n_pipe = lax.axis_size("pipe")
    n_tensor = lax.axis_size("tensor")
    group = n_pipe * n_tensor
    micro, rows, width = embeds.shape
    seq_len = rows * n_tensor
    heads_q = w_query.shape[2] // HD
    heads_kv = w_key.shape[2] // HD
    kv_width = heads_kv * HD
    n_tiles = heads_q // heads_kv + 2
    depth = w_out.shape[1]
    vocab_dev = head_weight.shape[1]
    n_out = 4
    out_width = width // n_out
    n_far = max(n_pipe, 2)
    cos_table, sin_table = rotary_tables(seq_len)
    dims = (n_pipe, n_tensor, micro, rows, width, heads_q, heads_kv, vocab_dev)
    bf16, f32 = jnp.bfloat16, jnp.float32
    dma = pltpu.SemaphoreType.DMA
    any_spec = pl.BlockSpec(memory_space=pl.ANY)
    vmem_spec = pl.BlockSpec(memory_space=pltpu.VMEM)
    stat_rows = round_up(3 * micro, 8)
    tot_rows = round_up(micro, 8)
    losses, scores = pl.pallas_call(
        functools.partial(relay_kernel, dims),
        out_shape=(
            jax.ShapeDtypeStruct((micro, seq_len), f32),
            jax.ShapeDtypeStruct((tot_rows, LANES), f32),
        ),
        in_specs=[any_spec, vmem_spec, vmem_spec] + [any_spec] * 4
        + [vmem_spec, any_spec, vmem_spec, vmem_spec],
        out_specs=(vmem_spec, vmem_spec),
        scratch_shapes=[
            pltpu.VMEM((n_tiles, width, kv_width), bf16),
            pltpu.VMEM((n_out, depth, out_width), bf16),
            pltpu.VMEM((width, vocab_dev), bf16),
            pltpu.VMEM((micro, n_out, rows, out_width), bf16),
            pltpu.VMEM((micro, n_tensor, rows, width), bf16),
            pltpu.VMEM((seq_len, width) if rows % 16 else (16, LANES), bf16),
            pltpu.VMEM((n_tiles, seq_len, kv_width), bf16),
            pltpu.VMEM((seq_len, depth), bf16),
            pltpu.VMEM((micro, n_out, n_tensor, rows, out_width), bf16),
            pltpu.VMEM((micro, n_out, n_tensor, rows, out_width), bf16),
            pltpu.VMEM((micro, n_out, rows, out_width), bf16),
            pltpu.VMEM((micro, n_tensor, rows, width), bf16),
            pltpu.VMEM((micro, seq_len, vocab_dev), f32),
            pltpu.VMEM((micro, seq_len, seq_len), f32),
            pltpu.VMEM((seq_len, LANES), f32),
            pltpu.VMEM((seq_len, LANES), f32),
            pltpu.VMEM((group, stat_rows, seq_len), f32),
            pltpu.VMEM((group, tot_rows, seq_len), f32),
            dma((n_tiles,)), dma((n_out,)), dma, dma((micro, n_out)),
            dma((micro, n_out)), dma((micro, n_out)),
            dma((micro, n_tensor)), dma((micro, n_tensor)),
            dma((micro, n_out, n_tensor)), dma((micro, n_out, n_tensor)),
            dma((micro, 2, n_far)), dma((micro, 2)),
            dma((micro, n_tensor)), dma((micro, n_tensor)),
            dma((group,)), dma((group,)), dma((group,)), dma((group,)),
        ],
        compiler_params=pltpu.CompilerParams(
            collective_id=0, has_side_effects=True, vmem_limit_bytes=58 * 1024 * 1024
        ),
    )(
        embeds, labels, norm_gain, w_query, w_key, w_value, w_out,
        final_gain.reshape(1, width), head_weight, jnp.asarray(cos_table), jnp.asarray(sin_table),
    )
    loss_width = seq_len // group
    device_slot = lax.axis_index("pipe") * n_tensor + lax.axis_index("tensor")
    token_loss = lax.dynamic_slice_in_dim(losses, device_slot * loss_width, loss_width, 1)
    return (token_loss, scores[:micro, 0])


def solution(mesh):
    in_specs = (
        P("dp", "tensor", None),
        P("dp", None),
        P("pipe", None),
        P("pipe", None, "tensor"),
        P("pipe", None, "tensor"),
        P("pipe", None, "tensor"),
        P("pipe", "tensor", None),
        P(),
        P(None, ("pipe", "tensor")),
    )
    out_specs = (P("dp", ("pipe", "tensor")), P("dp"))
    return jax.shard_map(
        per_device, mesh=mesh, in_specs=in_specs, out_specs=out_specs, check_vma=False
    )
```

```python
import functools
import math

import jax
import jax.numpy as jnp
import numpy as np
from jax import lax
from jax.experimental import pallas as pl
from jax.experimental.pallas import tpu as pltpu
from jax.sharding import PartitionSpec as P

HD = 128
EPSILON = 1e-05
ROPE_BASE = 500000.0
LANES = 128
MESH = pl.DeviceIdType.MESH
NEG = -1e30


def round_up(value, step):
    return (value + step - 1) // step * step


def rotary_tables(seq_len):
    half = HD // 2
    inverse = (ROPE_BASE ** (-2.0 * np.arange(half, dtype=np.float64) / HD)).astype(np.float32)
    angles = (np.arange(seq_len, dtype=np.float32)[:, None] * inverse[None, :]).astype(np.float64)
    cosine, sine = np.cos(angles), np.sin(angles)
    cos_table = np.concatenate([cosine, cosine], axis=1).astype(np.float32)
    sin_table = np.concatenate([-sine, sine], axis=1).astype(np.float32)
    return cos_table, sin_table


def relay_kernel(
    dims,
    embeds_ref, labels_ref, gain_ref, w_query_ref, w_key_ref, w_value_ref, w_out_ref,
    final_gain_ref, head_ref, cos_ref, sin_ref,
    loss_ref, score_ref,
    wqkv, wout, whead, full, acc, ctx, part, rs, outst, fin, logits, ghid,
    labcol, slab, stats, tots,
    w_sem, wo_sem, wh_sem, e_sem,
    in_send, in_recv, g_send, g_recv, r_send, r_recv,
    h_send, h_recv, s_send, s_recv, t_send, t_recv, u_send, u_recv,
):
    n_pipe, n_tensor, micro, rows, width, heads_q, heads_kv, vocab_dev, lag_in, lag_out = dims
    group = n_pipe * n_tensor
    seq_len = rows * n_tensor
    q_width, kv_width = heads_q * HD, heads_kv * HD
    per_kv = heads_q // heads_kv
    n_chunk, _, chunk = wout.shape
    last = n_pipe - 1
    p = lax.axis_index("pipe")
    t = lax.axis_index("tensor")
    slot = p * n_tensor + t
    near = [n_pipe - 2, n_pipe - 3] if n_pipe >= 3 else list(range(last))
    far = [q for q in range(last) if q not in near]

    def cols(n):
        return pl.ds(pl.multiple_of(n * chunk, chunk), chunk)

    def w_copies(n):
        q_at, k_at = q_width, q_width + kv_width
        pieces = ((w_query_ref, 0, q_at), (w_key_ref, q_at, k_at), (w_value_ref, k_at, k_at + kv_width))
        return [
            pltpu.make_async_copy(
                ref.at[0, cols(n), :], wqkv.at[n, :, pl.ds(lo, hi - lo)], w_sem.at[n, i]
            )
            for i, (ref, lo, hi) in enumerate(pieces)
        ]

    def wo_copy(n):
        return pltpu.make_async_copy(w_out_ref.at[0, :, cols(n)], wout.at[n], wo_sem.at[n])

    def e_copy(m, n):
        return pltpu.make_async_copy(embeds_ref.at[m, :, cols(n)], full.at[m, n, t], e_sem.at[m, n])

    head_copy = pltpu.make_async_copy(head_ref, whead, wh_sem)

    @pl.when(p == 0)
    def _():
        for m in range(micro):
            for n in range(n_chunk):
                e_copy(m, n).start()

    for n in range(n_chunk):
        for copy in w_copies(n):
            copy.start()

    @pl.when(p > 0)
    def _():
        for n in range(n_chunk):
            wo_copy(n).start()
        head_copy.start()

    def ring(j):
        peer = lax.rem(slot + j, group)
        return peer, {"pipe": peer // n_tensor, "tensor": lax.rem(peer, n_tensor)}

    barrier = pltpu.get_barrier_semaphore()
    for j in range(1, group):
        pl.semaphore_signal(barrier, inc=1, device_id=ring(j)[1], device_id_type=MESH)
    pl.semaphore_wait(barrier, group - 1)

    def remote(src, dst, send, recv, device):
        return pltpu.make_async_remote_copy(
            src_ref=src, dst_ref=dst, send_sem=send, recv_sem=recv,
            device_id=device, device_id_type=MESH,
        )

    def mate(j):
        return lax.rem(t + j, n_tensor)

    def in_copy(m, n):
        return remote(outst.at[m, n], full.at[m, n, t], in_send.at[m, n], in_recv.at[m, n],
                      {"pipe": lax.rem(p + 1, n_pipe)})

    def g_copy(m, n, j):
        return remote(full.at[m, n, t], full.at[m, n, t], g_send.at[m, n, j], g_recv.at[m, n, t],
                      {"tensor": mate(j)})

    def g_arrival(m, n, j):
        who = mate(j)
        return remote(full.at[m, n, who], full.at[m, n, who], g_send.at[m, n, j],
                      g_recv.at[m, n, who], {"tensor": who})

    def r_copy(m, n, j):
        who = mate(j)
        return remote(part.at[m, n, who], rs.at[m, n, t], r_send.at[m, n, j],
                      r_recv.at[m, n, t], {"tensor": who})

    def r_arrival(m, n, j):
        who = mate(j)
        return remote(part.at[m, n, who], rs.at[m, n, who], r_send.at[m, n, j],
                      r_recv.at[m, n, who], {"tensor": who})

    def h_copy(m, n, k, to):
        piece = fin.at[m, n, t]
        return remote(piece, piece, h_send.at[m, n, k], h_recv.at[m, n], {"pipe": to})

    def s_copy(m, n, j):
        return remote(fin.at[m, n, t], fin.at[m, n, t], s_send.at[m, n, j], s_recv.at[m, n, t],
                      {"tensor": mate(j)})

    def s_arrival(m, n, j):
        who = mate(j)
        return remote(fin.at[m, n, who], fin.at[m, n, who], s_send.at[m, n, j],
                      s_recv.at[m, n, who], {"tensor": who})

    def scaled(squares):
        return lax.rsqrt(squares * (1.0 / width) + EPSILON)

    row_at = lax.broadcasted_iota(jnp.int32, (per_kv * seq_len, seq_len), 0)
    key_at = lax.broadcasted_iota(jnp.int32, (per_kv * seq_len, seq_len), 1)
    causal = lax.rem(row_at, seq_len) >= key_at
    no_squares = jnp.zeros((seq_len, 1), jnp.float32)

    def layer(m, carry):
        def arrive(n):
            @pl.when(p > 0)
            def _():
                in_copy(m, n).wait_recv()

            @pl.when(p == 0)
            def _():
                e_copy(m, n).wait()

            for j in range(1, n_tensor):
                g_copy(m, n, j).start()

        acc[...] = jnp.zeros_like(acc)
        for n in range(lag_in):
            arrive(n)

        def project(n, squares):
            @pl.when(n + lag_in < n_chunk)
            def _():
                arrive(n + lag_in)

            for j in range(1, n_tensor):
                g_arrival(m, n, j).wait_recv()

            @pl.when(m == 0)
            def _():
                for copy in w_copies(n):
                    copy.wait()

            @pl.when((m == 0) & (p == 0) & (n == n_chunk - 2))
            def _():
                for i in range(n_chunk):
                    wo_copy(i).start()

            wide = full[m, n].astype(jnp.float32).reshape(seq_len, chunk)
            lhs = (wide * gain_ref[:, cols(n)]).astype(jnp.bfloat16)
            for at in range(0, q_width + 2 * kv_width, kv_width):
                acc[:, at : at + kv_width] += jnp.dot(
                    lhs, wqkv[n, :, at : at + kv_width], preferred_element_type=jnp.float32
                )
            return squares + jnp.sum(wide * wide, axis=-1, keepdims=True)

        factor = scaled(lax.fori_loop(0, n_chunk, project, no_squares))

        @pl.when((m == 0) & (p == 0))
        def _():
            head_copy.start()

        cosine, sine = cos_ref[...] * factor, sin_ref[...] * factor

        def turned(at):
            one = acc[:, at : at + HD]
            return (one * cosine + pltpu.roll(one, HD // 2, 1) * sine).astype(jnp.bfloat16)

        for h in range(heads_kv):
            queries = [turned((h * per_kv + g) * HD) for g in range(per_kv)]
            query = jnp.concatenate(queries, axis=0) if per_kv > 1 else queries[0]
            key = turned(q_width + h * HD)
            v_at = q_width + kv_width + h * HD
            value = (acc[:, v_at : v_at + HD] * factor).astype(jnp.bfloat16)
            scores = lax.dot_general(
                query, key, (((1,), (1,)), ((), ())), preferred_element_type=jnp.float32
            ) * (1.0 / math.sqrt(HD))
            scores = jnp.where(causal, scores, NEG)
            shifted = jnp.exp(scores - jnp.max(scores, axis=-1, keepdims=True))
            probs = (shifted / jnp.sum(shifted, axis=-1, keepdims=True)).astype(jnp.bfloat16)
            context = jnp.dot(probs, value, preferred_element_type=jnp.float32)
            for g in range(per_kv):
                at = (h * per_kv + g) * HD
                ctx[:, at : at + HD] = context[g * seq_len : (g + 1) * seq_len].astype(jnp.bfloat16)

        def combine(n):
            block = part[m, n, t].astype(jnp.float32)
            for j in range(1, n_tensor):
                r_arrival(m, n, j).wait_recv()
                block += rs[m, n, mate(j)].astype(jnp.float32)
            state = (full[m, n, t].astype(jnp.float32) + block).astype(jnp.bfloat16)

            @pl.when(p < last)
            def _():
                outst[m, n] = state
                in_copy(m, n).start()

            @pl.when(p == last)
            def _():
                fin[m, n, t] = state
                for k, to in enumerate(near):
                    h_copy(m, n, k, to).start()

        def output(n, c):
            @pl.when(m == 0)
            def _():
                wo_copy(n).wait()

            product = jnp.dot(ctx[...], wout[n], preferred_element_type=jnp.float32)
            part[m, n] = product.reshape(n_tensor, rows, chunk).astype(jnp.bfloat16)
            for j in range(1, n_tensor):
                r_copy(m, n, j).start()

            @pl.when(n >= lag_out)
            def _():
                combine(n - lag_out)

            return c

        lax.fori_loop(0, n_chunk, output, 0)
        for n in range(n_chunk - lag_out, n_chunk):
            combine(n)
        return carry

    lax.fori_loop(0, micro, layer, 0)

    pad = jnp.zeros((LANES - micro, seq_len), jnp.float32)
    labcol[...] = jnp.concatenate([labels_ref[...].astype(jnp.float32), pad], axis=0).T
    slab[...] = jnp.zeros_like(slab)
    lane = lax.broadcasted_iota(jnp.int32, (seq_len, LANES), 1)
    entry = (lax.broadcasted_iota(jnp.int32, (seq_len, vocab_dev), 1) + slot * vocab_dev).astype(
        jnp.float32
    )
    head_copy.wait()

    def head(m, carry):
        def arrive(n):
            @pl.when(p < last)
            def _():
                h_copy(m, n, 0, last).wait_recv()

            if far:
                for k in range(2):
                    @pl.when((p == near[k]) & (lax.rem(n, 2) == k))
                    def _():
                        for f, to in enumerate(far):
                            h_copy(m, n, f, to).start()

            for j in range(1, n_tensor):
                s_copy(m, n, j).start()

        logits[m] = jnp.zeros_like(logits[m])
        ghid[m] = jnp.zeros_like(ghid[m])
        for n in range(lag_in):
            arrive(n)

        def score(n, squares):
            @pl.when(n + lag_in < n_chunk)
            def _():
                arrive(n + lag_in)

            for j in range(1, n_tensor):
                s_arrival(m, n, j).wait_recv()
            wide = fin[m, n].astype(jnp.float32).reshape(seq_len, chunk)
            lhs = (wide * final_gain_ref[:, cols(n)]).astype(jnp.bfloat16)
            logits[m] += jnp.dot(lhs, whead[cols(n), :], preferred_element_type=jnp.float32)
            ghid[m] += lax.dot_general(
                lhs, lhs, (((1,), (1,)), ((), ())), preferred_element_type=jnp.float32
            )
            return squares + jnp.sum(wide * wide, axis=-1, keepdims=True)

        factor = scaled(lax.fori_loop(0, n_chunk, score, no_squares))
        local = logits[m] * factor
        logits[m] = local
        own = jnp.sum(jnp.where(lane == m, labcol[...], 0.0), axis=-1, keepdims=True)
        peak = jnp.max(local, axis=-1, keepdims=True)
        mass = jnp.sum(jnp.exp(local - peak), axis=-1, keepdims=True)
        target = jnp.sum(jnp.where(entry == own, local, 0.0), axis=-1, keepdims=True)
        kept = slab[...]
        for i, column in enumerate((peak, mass, target, factor)):
            kept = jnp.where(lane == i * micro + m, column, kept)
        slab[...] = kept
        return carry

    lax.fori_loop(0, micro, head, 0)

    n_stats = stats.shape[1]
    slab_cols = slab[...]
    stats[slot] = slab_cols.T[:n_stats]

    def exchange(buffer, send, recv):
        def copy(j):
            peer, device = ring(j)
            return remote(buffer.at[slot], buffer.at[slot], send.at[j], recv.at[slot], device)

        def arrival(j):
            peer, device = ring(j)
            return remote(buffer.at[peer], buffer.at[peer], send.at[j], recv.at[peer], device)

        for j in range(1, group):
            copy(j).start()
        for j in range(1, group):
            arrival(j).wait_recv()
        return copy

    stats_copy = exchange(stats, t_send, t_recv)
    peaks = stats[:, :micro, :]
    peak_row = jnp.max(peaks, axis=0)
    masses = jnp.exp(peaks - peak_row[None]) * stats[:, micro : 2 * micro, :]
    log_norm = peak_row + jnp.log(jnp.sum(masses, axis=0))
    loss_ref[...] = log_norm - jnp.sum(stats[:, 2 * micro : 3 * micro, :], axis=0)
    factor_rows = stats[0, 3 * micro : 4 * micro, :]
    labels_t = labcol[...]
    norm_t = jnp.concatenate([log_norm, pad], axis=0).T

    tot_rows = tots.shape[1]
    row_id = lax.broadcasted_iota(jnp.int32, (tot_rows, seq_len), 0)
    sums = jnp.zeros((tot_rows, seq_len), jnp.float32)
    for m in range(micro):
        onehot = (entry == labels_t[:, m : m + 1]).astype(jnp.float32)
        errors = (jnp.exp(logits[m] - norm_t[:, m : m + 1]) - onehot).astype(jnp.bfloat16)
        gram = lax.dot_general(
            errors, errors, (((1,), (1,)), ((), ())), preferred_element_type=jnp.float32
        )
        f_at = 3 * micro + m
        weighted = gram * ghid[m] * slab_cols[:, f_at : f_at + 1]
        row = jnp.sum(weighted, axis=0, keepdims=True) * factor_rows[m : m + 1]
        sums = jnp.where(row_id == m, row, sums)
    tots[slot] = sums
    tots_copy = exchange(tots, u_send, u_recv)
    total = jnp.sum(jnp.sum(tots[...], axis=0), axis=-1, keepdims=True)
    score_ref[...] = jnp.broadcast_to(jnp.sqrt(total) / seq_len, score_ref.shape)

    def drain(m, carry):
        for n in range(n_chunk):
            for j in range(1, n_tensor):
                g_copy(m, n, j).wait_send()
                s_copy(m, n, j).wait_send()
                r_copy(m, n, j).wait_send()

        @pl.when(p < last)
        def _():
            for n in range(n_chunk):
                in_copy(m, n).wait_send()

        @pl.when(p == last)
        def _():
            for n in range(n_chunk):
                for k, to in enumerate(near):
                    h_copy(m, n, k, to).wait_send()

        if far:
            for k in range(2):
                @pl.when(p == near[k])
                def _():
                    for n in range(k, n_chunk, 2):
                        for f, to in enumerate(far):
                            h_copy(m, n, f, to).wait_send()

        return carry

    lax.fori_loop(0, micro, drain, 0)
    for j in range(1, group):
        stats_copy(j).wait_send()
        tots_copy(j).wait_send()


def per_device(embeds, labels, norm_gain, w_query, w_key, w_value, w_out, final_gain, head_weight):
    n_pipe = lax.axis_size("pipe")
    n_tensor = lax.axis_size("tensor")
    group = n_pipe * n_tensor
    micro, rows, width = embeds.shape
    seq_len = rows * n_tensor
    heads_q = w_query.shape[2] // HD
    heads_kv = w_key.shape[2] // HD
    qkv_width = (heads_q + 2 * heads_kv) * HD
    depth = w_out.shape[1]
    vocab_dev = head_weight.shape[1]
    n_chunk, lag_in, lag_out = 4, 1, 2
    chunk = width // n_chunk
    n_far = max(n_pipe, 2)
    cos_table, sin_table = rotary_tables(seq_len)
    dims = (n_pipe, n_tensor, micro, rows, width, heads_q, heads_kv, vocab_dev, lag_in, lag_out)
    bf16, f32 = jnp.bfloat16, jnp.float32
    dma = pltpu.SemaphoreType.DMA
    any_spec = pl.BlockSpec(memory_space=pl.ANY)
    vmem_spec = pl.BlockSpec(memory_space=pltpu.VMEM)
    stat_rows = round_up(4 * micro, 8)
    tot_rows = round_up(micro, 8)
    losses, scores = pl.pallas_call(
        functools.partial(relay_kernel, dims),
        out_shape=(
            jax.ShapeDtypeStruct((micro, seq_len), f32),
            jax.ShapeDtypeStruct((tot_rows, LANES), f32),
        ),
        in_specs=[any_spec, vmem_spec, vmem_spec] + [any_spec] * 4
        + [vmem_spec, any_spec, vmem_spec, vmem_spec],
        out_specs=(vmem_spec, vmem_spec),
        scratch_shapes=[
            pltpu.VMEM((n_chunk, chunk, qkv_width), bf16),
            pltpu.VMEM((n_chunk, depth, chunk), bf16),
            pltpu.VMEM((width, vocab_dev), bf16),
            pltpu.VMEM((micro, n_chunk, n_tensor, rows, chunk), bf16),
            pltpu.VMEM((seq_len, qkv_width), f32),
            pltpu.VMEM((seq_len, depth), bf16),
            pltpu.VMEM((micro, n_chunk, n_tensor, rows, chunk), bf16),
            pltpu.VMEM((micro, n_chunk, n_tensor, rows, chunk), bf16),
            pltpu.VMEM((micro, n_chunk, rows, chunk), bf16),
            pltpu.VMEM((micro, n_chunk, n_tensor, rows, chunk), bf16),
            pltpu.VMEM((micro, seq_len, vocab_dev), f32),
            pltpu.VMEM((micro, seq_len, seq_len), f32),
            pltpu.VMEM((seq_len, LANES), f32),
            pltpu.VMEM((seq_len, LANES), f32),
            pltpu.VMEM((group, stat_rows, seq_len), f32),
            pltpu.VMEM((group, tot_rows, seq_len), f32),
            dma((n_chunk, 3)), dma((n_chunk,)), dma, dma((micro, n_chunk)),
            dma((micro, n_chunk)), dma((micro, n_chunk)),
            dma((micro, n_chunk, n_tensor)), dma((micro, n_chunk, n_tensor)),
            dma((micro, n_chunk, n_tensor)), dma((micro, n_chunk, n_tensor)),
            dma((micro, n_chunk, n_far)), dma((micro, n_chunk)),
            dma((micro, n_chunk, n_tensor)), dma((micro, n_chunk, n_tensor)),
            dma((group,)), dma((group,)), dma((group,)), dma((group,)),
        ],
        compiler_params=pltpu.CompilerParams(
            collective_id=0, has_side_effects=True, vmem_limit_bytes=58 * 1024 * 1024
        ),
    )(
        embeds, labels, norm_gain, w_query, w_key, w_value, w_out,
        final_gain.reshape(1, width), head_weight, jnp.asarray(cos_table), jnp.asarray(sin_table),
    )
    loss_width = seq_len // group
    device_slot = lax.axis_index("pipe") * n_tensor + lax.axis_index("tensor")
    token_loss = lax.dynamic_slice_in_dim(losses, device_slot * loss_width, loss_width, 1)
    return (token_loss, scores[:micro, 0])


def solution(mesh):
    in_specs = (
        P("dp", "tensor", None),
        P("dp", None),
        P("pipe", None),
        P("pipe", None, "tensor"),
        P("pipe", None, "tensor"),
        P("pipe", None, "tensor"),
        P("pipe", "tensor", None),
        P(),
        P(None, ("pipe", "tensor")),
    )
    out_specs = (P("dp", ("pipe", "tensor")), P("dp"))
    return jax.shard_map(
        per_device, mesh=mesh, in_specs=in_specs, out_specs=out_specs, check_vma=False
    )
```

```python
import functools
import math

import jax
import jax.numpy as jnp
import numpy as np
from jax import lax
from jax.experimental import pallas as pl
from jax.experimental.pallas import tpu as pltpu
from jax.sharding import PartitionSpec as P

HD = 128
EPSILON = 1e-05
ROPE_BASE = 500000.0
LANES = 128
MESH = pl.DeviceIdType.MESH
NEG = -1e30


def round_up(value, step):
    return (value + step - 1) // step * step


def rotary_tables(seq_len):
    half = HD // 2
    inverse = (ROPE_BASE ** (-2.0 * np.arange(half, dtype=np.float64) / HD)).astype(np.float32)
    angles = (np.arange(seq_len, dtype=np.float32)[:, None] * inverse[None, :]).astype(np.float64)
    cosine, sine = np.cos(angles), np.sin(angles)
    cos_table = np.concatenate([cosine, cosine], axis=1).astype(np.float32)
    sin_table = np.concatenate([-sine, sine], axis=1).astype(np.float32)
    return cos_table, sin_table


def relay_kernel(
    dims,
    embeds_ref, labels_ref, gain_ref, w_query_ref, w_key_ref, w_value_ref, w_out_ref,
    final_gain_ref, head_ref, cos_ref, sin_ref,
    loss_ref, score_ref,
    wqkv, wout, whead, full, acc, ctx, part, rs, outst, fin, logits, ghid,
    labcol, slab, stats, tots,
    w_sem, wo_sem, wh_sem, e_sem,
    in_send, in_recv, g_send, g_recv, r_send, r_recv,
    h_send, h_recv, s_send, s_recv, t_send, t_recv, u_send, u_recv,
):
    n_pipe, n_tensor, micro, batch, own_rows, width, heads_q, heads_kv, vocab_dev, lag_in, lag_out = dims
    group = n_pipe * n_tensor
    rows = batch * own_rows
    seq_len = own_rows * n_tensor
    step_len = rows * n_tensor
    q_width, kv_width = heads_q * HD, heads_kv * HD
    per_kv = heads_q // heads_kv
    n_chunk, _, chunk = wout.shape
    last = n_pipe - 1
    p = lax.axis_index("pipe")
    t = lax.axis_index("tensor")
    slot = p * n_tensor + t
    near = [n_pipe - 2, n_pipe - 3] if n_pipe >= 3 else list(range(last))
    far = [q for q in range(last) if q not in near]

    def cols(n):
        return pl.ds(pl.multiple_of(n * chunk, chunk), chunk)

    def w_copies(n):
        q_at, k_at = q_width, q_width + kv_width
        pieces = ((w_query_ref, 0, q_at), (w_key_ref, q_at, k_at), (w_value_ref, k_at, k_at + kv_width))
        return [
            pltpu.make_async_copy(
                ref.at[0, cols(n), :], wqkv.at[n, :, pl.ds(lo, hi - lo)], w_sem.at[n, i]
            )
            for i, (ref, lo, hi) in enumerate(pieces)
        ]

    def wo_copy(n):
        return pltpu.make_async_copy(w_out_ref.at[0, :, cols(n)], wout.at[n], wo_sem.at[n])

    def e_copy(m, n):
        return pltpu.make_async_copy(embeds_ref.at[m, :, cols(n)], full.at[m, n, t], e_sem.at[m, n])

    head_copy = pltpu.make_async_copy(head_ref, whead, wh_sem)

    @pl.when(p == 0)
    def _():
        for m in range(micro):
            for n in range(n_chunk):
                e_copy(m, n).start()

    for n in range(n_chunk):
        for copy in w_copies(n):
            copy.start()

    @pl.when(p > 0)
    def _():
        for n in range(n_chunk):
            wo_copy(n).start()
        head_copy.start()

    def ring(j):
        peer = lax.rem(slot + j, group)
        return peer, {"pipe": peer // n_tensor, "tensor": lax.rem(peer, n_tensor)}

    barrier = pltpu.get_barrier_semaphore()
    for j in range(1, group):
        pl.semaphore_signal(barrier, inc=1, device_id=ring(j)[1], device_id_type=MESH)
    pl.semaphore_wait(barrier, group - 1)

    def remote(src, dst, send, recv, device):
        return pltpu.make_async_remote_copy(
            src_ref=src, dst_ref=dst, send_sem=send, recv_sem=recv,
            device_id=device, device_id_type=MESH,
        )

    def mate(j):
        return lax.rem(t + j, n_tensor)

    def in_copy(m, n):
        return remote(outst.at[m, n], full.at[m, n, t], in_send.at[m, n], in_recv.at[m, n],
                      {"pipe": lax.rem(p + 1, n_pipe)})

    def g_copy(m, n, j):
        return remote(full.at[m, n, t], full.at[m, n, t], g_send.at[m, n, j], g_recv.at[m, n, t],
                      {"tensor": mate(j)})

    def g_arrival(m, n, j):
        who = mate(j)
        return remote(full.at[m, n, who], full.at[m, n, who], g_send.at[m, n, j],
                      g_recv.at[m, n, who], {"tensor": who})

    def r_copy(m, n, j):
        who = mate(j)
        return remote(part.at[m, n, who], rs.at[m, n, t], r_send.at[m, n, j],
                      r_recv.at[m, n, t], {"tensor": who})

    def r_arrival(m, n, j):
        who = mate(j)
        return remote(part.at[m, n, who], rs.at[m, n, who], r_send.at[m, n, j],
                      r_recv.at[m, n, who], {"tensor": who})

    def h_copy(m, n, k, to):
        piece = fin.at[m, n, t]
        return remote(piece, piece, h_send.at[m, n, k], h_recv.at[m, n], {"pipe": to})

    def s_copy(m, n, j):
        return remote(fin.at[m, n, t], fin.at[m, n, t], s_send.at[m, n, j], s_recv.at[m, n, t],
                      {"tensor": mate(j)})

    def s_arrival(m, n, j):
        who = mate(j)
        return remote(fin.at[m, n, who], fin.at[m, n, who], s_send.at[m, n, j],
                      s_recv.at[m, n, who], {"tensor": who})

    def scaled(squares):
        return lax.rsqrt(squares * (1.0 / width) + EPSILON)

    row_at = lax.broadcasted_iota(jnp.int32, (per_kv * seq_len, seq_len), 0)
    key_at = lax.broadcasted_iota(jnp.int32, (per_kv * seq_len, seq_len), 1)
    causal = lax.rem(row_at, seq_len) >= key_at
    no_squares = jnp.zeros((step_len, 1), jnp.float32)

    def layer(m, carry):
        def arrive(n):
            @pl.when(p > 0)
            def _():
                in_copy(m, n).wait_recv()

            @pl.when(p == 0)
            def _():
                e_copy(m, n).wait()

            for j in range(1, n_tensor):
                g_copy(m, n, j).start()

        acc[...] = jnp.zeros_like(acc)
        for n in range(lag_in):
            arrive(n)

        def project(n, squares):
            @pl.when(n + lag_in < n_chunk)
            def _():
                arrive(n + lag_in)

            for j in range(1, n_tensor):
                g_arrival(m, n, j).wait_recv()

            @pl.when(m == 0)
            def _():
                for copy in w_copies(n):
                    copy.wait()

            @pl.when((m == 0) & (p == 0) & (n == n_chunk - 2))
            def _():
                for i in range(n_chunk):
                    wo_copy(i).start()

            wide = full[m, n].astype(jnp.float32).reshape(step_len, chunk)
            lhs = (wide * gain_ref[:, cols(n)]).astype(jnp.bfloat16)
            for at in range(0, q_width + 2 * kv_width, kv_width):
                acc[:, at : at + kv_width] += jnp.dot(
                    lhs, wqkv[n, :, at : at + kv_width], preferred_element_type=jnp.float32
                )
            return squares + jnp.sum(wide * wide, axis=-1, keepdims=True)

        factor = scaled(lax.fori_loop(0, n_chunk, project, no_squares))

        @pl.when((m == 0) & (p == 0))
        def _():
            head_copy.start()

        def of_sequence(value, b):
            starts = [i * rows + b * own_rows for i in range(n_tensor)]
            return jnp.concatenate([value[at : at + own_rows] for at in starts], axis=0)

        def attend(b):
            own_factor = of_sequence(factor, b)
            cosine, sine = cos_ref[...] * own_factor, sin_ref[...] * own_factor

            def head_of(at):
                starts = [i * rows + b * own_rows for i in range(n_tensor)]
                return jnp.concatenate(
                    [acc[lo : lo + own_rows, at : at + HD] for lo in starts], axis=0
                )

            def turned(at):
                one = head_of(at)
                return (one * cosine + pltpu.roll(one, HD // 2, 1) * sine).astype(jnp.bfloat16)

            for h in range(heads_kv):
                queries = [turned((h * per_kv + g) * HD) for g in range(per_kv)]
                query = jnp.concatenate(queries, axis=0) if per_kv > 1 else queries[0]
                key = turned(q_width + h * HD)
                value = (head_of(q_width + kv_width + h * HD) * own_factor).astype(jnp.bfloat16)
                scores = lax.dot_general(
                    query, key, (((1,), (1,)), ((), ())), preferred_element_type=jnp.float32
                ) * (1.0 / math.sqrt(HD))
                scores = jnp.where(causal, scores, NEG)
                shifted = jnp.exp(scores - jnp.max(scores, axis=-1, keepdims=True))
                probs = (shifted / jnp.sum(shifted, axis=-1, keepdims=True)).astype(jnp.bfloat16)
                context = jnp.dot(probs, value, preferred_element_type=jnp.float32)
                for g in range(per_kv):
                    at = (h * per_kv + g) * HD
                    for i in range(n_tensor):
                        lo, frm = i * rows + b * own_rows, g * seq_len + i * own_rows
                        ctx[lo : lo + own_rows, at : at + HD] = context[
                            frm : frm + own_rows
                        ].astype(jnp.bfloat16)

        for b in range(batch):
            attend(b)

        def combine(n):
            block = part[m, n, t].astype(jnp.float32)
            for j in range(1, n_tensor):
                r_arrival(m, n, j).wait_recv()
                block += rs[m, n, mate(j)].astype(jnp.float32)
            state = (full[m, n, t].astype(jnp.float32) + block).astype(jnp.bfloat16)

            @pl.when(p < last)
            def _():
                outst[m, n] = state
                in_copy(m, n).start()

            @pl.when(p == last)
            def _():
                fin[m, n, t] = state
                for k, to in enumerate(near):
                    h_copy(m, n, k, to).start()

        def output(n, c):
            @pl.when(m == 0)
            def _():
                wo_copy(n).wait()

            product = jnp.dot(ctx[...], wout[n], preferred_element_type=jnp.float32)
            part[m, n] = product.reshape(n_tensor, rows, chunk).astype(jnp.bfloat16)
            for j in range(1, n_tensor):
                r_copy(m, n, j).start()

            @pl.when(n >= lag_out)
            def _():
                combine(n - lag_out)

            return c

        lax.fori_loop(0, n_chunk, output, 0)
        for n in range(n_chunk - lag_out, n_chunk):
            combine(n)
        return carry

    lax.fori_loop(0, micro, layer, 0)

    lab_pad = jnp.zeros((LANES - micro * batch, seq_len), jnp.float32)
    lab = jnp.concatenate([labels_ref[...].astype(jnp.float32), lab_pad], axis=0).T
    few = lax.broadcasted_iota(jnp.int32, (own_rows, LANES), 1)
    for i in range(n_tensor):
        for b in range(batch):
            block = jnp.zeros((own_rows, LANES), jnp.float32)
            for m in range(micro):
                at = m * batch + b
                column = lab[i * own_rows : (i + 1) * own_rows, at : at + 1]
                block = jnp.where(few == m, column, block)
            lo = i * rows + b * own_rows
            labcol[lo : lo + own_rows, :] = block
    slab[...] = jnp.zeros_like(slab)
    lane = lax.broadcasted_iota(jnp.int32, (step_len, LANES), 1)
    entry = (lax.broadcasted_iota(jnp.int32, (step_len, vocab_dev), 1) + slot * vocab_dev).astype(
        jnp.float32
    )
    head_copy.wait()

    def head(m, carry):
        def arrive(n):
            @pl.when(p < last)
            def _():
                h_copy(m, n, 0, last).wait_recv()

            if far:
                for k in range(2):
                    @pl.when((p == near[k]) & (lax.rem(n, 2) == k))
                    def _():
                        for f, to in enumerate(far):
                            h_copy(m, n, f, to).start()

            for j in range(1, n_tensor):
                s_copy(m, n, j).start()

        logits[m] = jnp.zeros_like(logits[m])
        ghid[m] = jnp.zeros_like(ghid[m])
        for n in range(lag_in):
            arrive(n)

        def score(n, squares):
            @pl.when(n + lag_in < n_chunk)
            def _():
                arrive(n + lag_in)

            for j in range(1, n_tensor):
                s_arrival(m, n, j).wait_recv()
            wide = fin[m, n].astype(jnp.float32).reshape(step_len, chunk)
            lhs = (wide * final_gain_ref[:, cols(n)]).astype(jnp.bfloat16)
            logits[m] += jnp.dot(lhs, whead[cols(n), :], preferred_element_type=jnp.float32)
            ghid[m] += lax.dot_general(
                lhs, lhs, (((1,), (1,)), ((), ())), preferred_element_type=jnp.float32
            )
            return squares + jnp.sum(wide * wide, axis=-1, keepdims=True)

        factor = scaled(lax.fori_loop(0, n_chunk, score, no_squares))
        local = logits[m] * factor
        logits[m] = local
        own = jnp.sum(jnp.where(lane == m, labcol[...], 0.0), axis=-1, keepdims=True)
        peak = jnp.max(local, axis=-1, keepdims=True)
        mass = jnp.sum(jnp.exp(local - peak), axis=-1, keepdims=True)
        target = jnp.sum(jnp.where(entry == own, local, 0.0), axis=-1, keepdims=True)
        kept = slab[...]
        for i, column in enumerate((peak, mass, target, factor)):
            kept = jnp.where(lane == i * micro + m, column, kept)
        slab[...] = kept
        return carry

    lax.fori_loop(0, micro, head, 0)

    n_stats = stats.shape[1]
    slab_cols = slab[...]
    stats[slot] = slab_cols.T[:n_stats]

    def exchange(buffer, send, recv):
        def copy(j):
            peer, device = ring(j)
            return remote(buffer.at[slot], buffer.at[slot], send.at[j], recv.at[slot], device)

        def arrival(j):
            peer, device = ring(j)
            return remote(buffer.at[peer], buffer.at[peer], send.at[j], recv.at[peer], device)

        for j in range(1, group):
            copy(j).start()
        for j in range(1, group):
            arrival(j).wait_recv()
        return copy

    stats_copy = exchange(stats, t_send, t_recv)
    peaks = stats[:, :micro, :]
    peak_row = jnp.max(peaks, axis=0)
    masses = jnp.exp(peaks - peak_row[None]) * stats[:, micro : 2 * micro, :]
    log_norm = peak_row + jnp.log(jnp.sum(masses, axis=0))
    loss_ref[...] = log_norm - jnp.sum(stats[:, 2 * micro : 3 * micro, :], axis=0)
    factor_rows = stats[0, 3 * micro : 4 * micro, :]
    labels_t = labcol[...]
    pad = jnp.zeros((LANES - micro, step_len), jnp.float32)
    norm_t = jnp.concatenate([log_norm, pad], axis=0).T

    def sequence_at(shape, dim):
        return lax.rem(lax.div(lax.broadcasted_iota(jnp.int32, shape, dim), own_rows), batch)

    square = (step_len, step_len)
    same = sequence_at(square, 0) == sequence_at(square, 1)

    tot_rows = tots.shape[1]
    row_id = lax.broadcasted_iota(jnp.int32, (tot_rows, step_len), 0)
    sums = jnp.zeros((tot_rows, step_len), jnp.float32)
    for m in range(micro):
        onehot = (entry == labels_t[:, m : m + 1]).astype(jnp.float32)
        errors = (jnp.exp(logits[m] - norm_t[:, m : m + 1]) - onehot).astype(jnp.bfloat16)
        gram = lax.dot_general(
            errors, errors, (((1,), (1,)), ((), ())), preferred_element_type=jnp.float32
        )
        f_at = 3 * micro + m
        weighted = jnp.where(same, gram * ghid[m] * slab_cols[:, f_at : f_at + 1], 0.0)
        row = jnp.sum(weighted, axis=0, keepdims=True) * factor_rows[m : m + 1]
        sums = jnp.where(row_id == m, row, sums)
    tots[slot] = sums
    tots_copy = exchange(tots, u_send, u_recv)
    total = jnp.sum(tots[...], axis=0)
    of_row = sequence_at((tot_rows, step_len), 1)
    out_lane = lax.broadcasted_iota(jnp.int32, score_ref.shape, 1)
    scored = jnp.zeros(score_ref.shape, jnp.float32)
    for b in range(batch):
        own = jnp.sum(jnp.where(of_row == b, total, 0.0), axis=-1, keepdims=True)
        scored = jnp.where(out_lane == b, jnp.sqrt(own) / seq_len, scored)
    score_ref[...] = scored

    def drain(m, carry):
        for n in range(n_chunk):
            for j in range(1, n_tensor):
                g_copy(m, n, j).wait_send()
                s_copy(m, n, j).wait_send()
                r_copy(m, n, j).wait_send()

        @pl.when(p < last)
        def _():
            for n in range(n_chunk):
                in_copy(m, n).wait_send()

        @pl.when(p == last)
        def _():
            for n in range(n_chunk):
                for k, to in enumerate(near):
                    h_copy(m, n, k, to).wait_send()

        if far:
            for k in range(2):
                @pl.when(p == near[k])
                def _():
                    for n in range(k, n_chunk, 2):
                        for f, to in enumerate(far):
                            h_copy(m, n, f, to).wait_send()

        return carry

    lax.fori_loop(0, micro, drain, 0)
    for j in range(1, group):
        stats_copy(j).wait_send()
        tots_copy(j).wait_send()


def per_device(embeds, labels, norm_gain, w_query, w_key, w_value, w_out, final_gain, head_weight):
    n_pipe = lax.axis_size("pipe")
    n_tensor = lax.axis_size("tensor")
    group = n_pipe * n_tensor
    sequences, own_rows, width = embeds.shape
    seq_len = own_rows * n_tensor
    batch = 2 if sequences % 2 == 0 else 1
    micro, rows = sequences // batch, batch * own_rows
    step_len = rows * n_tensor
    heads_q = w_query.shape[2] // HD
    heads_kv = w_key.shape[2] // HD
    qkv_width = (heads_q + 2 * heads_kv) * HD
    depth = w_out.shape[1]
    vocab_dev = head_weight.shape[1]
    n_chunk, lag_in, lag_out = 8, 2, 3
    chunk = width // n_chunk
    n_far = max(n_pipe, 2)
    cos_table, sin_table = rotary_tables(seq_len)
    dims = (n_pipe, n_tensor, micro, batch, own_rows, width, heads_q, heads_kv, vocab_dev, lag_in, lag_out)
    bf16, f32 = jnp.bfloat16, jnp.float32
    dma = pltpu.SemaphoreType.DMA
    any_spec = pl.BlockSpec(memory_space=pl.ANY)
    vmem_spec = pl.BlockSpec(memory_space=pltpu.VMEM)
    stat_rows = round_up(4 * micro, 8)
    tot_rows = round_up(micro, 8)
    losses, scores = pl.pallas_call(
        functools.partial(relay_kernel, dims),
        out_shape=(
            jax.ShapeDtypeStruct((micro, step_len), f32),
            jax.ShapeDtypeStruct((tot_rows, LANES), f32),
        ),
        in_specs=[any_spec, vmem_spec, vmem_spec] + [any_spec] * 4
        + [vmem_spec, any_spec, vmem_spec, vmem_spec],
        out_specs=(vmem_spec, vmem_spec),
        scratch_shapes=[
            pltpu.VMEM((n_chunk, chunk, qkv_width), bf16),
            pltpu.VMEM((n_chunk, depth, chunk), bf16),
            pltpu.VMEM((width, vocab_dev), bf16),
            pltpu.VMEM((micro, n_chunk, n_tensor, rows, chunk), bf16),
            pltpu.VMEM((step_len, qkv_width), f32),
            pltpu.VMEM((step_len, depth), bf16),
            pltpu.VMEM((micro, n_chunk, n_tensor, rows, chunk), bf16),
            pltpu.VMEM((micro, n_chunk, n_tensor, rows, chunk), bf16),
            pltpu.VMEM((micro, n_chunk, rows, chunk), bf16),
            pltpu.VMEM((micro, n_chunk, n_tensor, rows, chunk), bf16),
            pltpu.VMEM((micro, step_len, vocab_dev), f32),
            pltpu.VMEM((micro, step_len, step_len), f32),
            pltpu.VMEM((step_len, LANES), f32),
            pltpu.VMEM((step_len, LANES), f32),
            pltpu.VMEM((group, stat_rows, step_len), f32),
            pltpu.VMEM((group, tot_rows, step_len), f32),
            dma((n_chunk, 3)), dma((n_chunk,)), dma, dma((micro, n_chunk)),
            dma((micro, n_chunk)), dma((micro, n_chunk)),
            dma((micro, n_chunk, n_tensor)), dma((micro, n_chunk, n_tensor)),
            dma((micro, n_chunk, n_tensor)), dma((micro, n_chunk, n_tensor)),
            dma((micro, n_chunk, n_far)), dma((micro, n_chunk)),
            dma((micro, n_chunk, n_tensor)), dma((micro, n_chunk, n_tensor)),
            dma((group,)), dma((group,)), dma((group,)), dma((group,)),
        ],
        compiler_params=pltpu.CompilerParams(
            collective_id=0, has_side_effects=True, vmem_limit_bytes=58 * 1024 * 1024
        ),
    )(
        embeds.reshape(micro, rows, width), labels, norm_gain, w_query, w_key, w_value, w_out,
        final_gain.reshape(1, width), head_weight, jnp.asarray(cos_table), jnp.asarray(sin_table),
    )
    loss_width = seq_len // group
    device_slot = lax.axis_index("pipe") * n_tensor + lax.axis_index("tensor")
    losses = losses.reshape(micro, n_tensor, batch, own_rows).transpose(0, 2, 1, 3)
    losses = losses.reshape(sequences, seq_len)
    token_loss = lax.dynamic_slice_in_dim(losses, device_slot * loss_width, loss_width, 1)
    return (token_loss, scores[:micro, :batch].reshape(sequences))


def solution(mesh):
    in_specs = (
        P("dp", "tensor", None),
        P("dp", None),
        P("pipe", None),
        P("pipe", None, "tensor"),
        P("pipe", None, "tensor"),
        P("pipe", None, "tensor"),
        P("pipe", "tensor", None),
        P(),
        P(None, ("pipe", "tensor")),
    )
    out_specs = (P("dp", ("pipe", "tensor")), P("dp"))
    return jax.shard_map(
        per_device, mesh=mesh, in_specs=in_specs, out_specs=out_specs, check_vma=False
    )
```

```python
import functools
import math

import jax
import jax.numpy as jnp
import numpy as np
from jax import lax
from jax.experimental import pallas as pl
from jax.experimental.pallas import tpu as pltpu
from jax.sharding import PartitionSpec as P

HD = 128
EPSILON = 1e-05
ROPE_BASE = 500000.0
LANES = 128
MESH = pl.DeviceIdType.MESH
NEG = -1e30


def round_up(value, step):
    return (value + step - 1) // step * step


def rotary_tables(seq_len):
    half = HD // 2
    inverse = (ROPE_BASE ** (-2.0 * np.arange(half, dtype=np.float64) / HD)).astype(np.float32)
    angles = (np.arange(seq_len, dtype=np.float32)[:, None] * inverse[None, :]).astype(np.float64)
    cosine, sine = np.cos(angles), np.sin(angles)
    cos_table = np.concatenate([cosine, cosine], axis=1).astype(np.float32)
    sin_table = np.concatenate([-sine, sine], axis=1).astype(np.float32)
    return cos_table, sin_table


def relay_kernel(
    dims,
    embeds_ref, labels_ref, gain_ref, w_query_ref, w_key_ref, w_value_ref, w_out_ref,
    final_gain_ref, head_ref, cos_ref, sin_ref,
    loss_ref, score_ref,
    wqkv, wout, whead, full, acc, ctx, part, rs, outst, fin, logits, ghid,
    labcol, slab, stats, tots,
    w_sem, wo_sem, wh_sem, e_sem,
    in_send, in_recv, g_send, g_recv, r_send, r_recv,
    h_send, h_recv, s_send, s_recv, t_send, t_recv, u_send, u_recv,
):
    n_pipe, n_tensor, micro, batch, own_rows, width, heads_q, heads_kv, vocab_dev, lag_in, lag_out = dims
    group = n_pipe * n_tensor
    rows = batch * own_rows
    seq_len = own_rows * n_tensor
    step_len = rows * n_tensor
    q_width, kv_width = heads_q * HD, heads_kv * HD
    per_kv = heads_q // heads_kv
    n_chunk, _, chunk = wout.shape
    last = n_pipe - 1
    p = lax.axis_index("pipe")
    t = lax.axis_index("tensor")
    slot = p * n_tensor + t
    near = [n_pipe - 2, n_pipe - 3] if n_pipe >= 3 else list(range(last))
    far = [q for q in range(last) if q not in near]

    def cols(n):
        return pl.ds(pl.multiple_of(n * chunk, chunk), chunk)

    def w_copies(n):
        q_at, k_at = q_width, q_width + kv_width
        pieces = ((w_query_ref, 0, q_at), (w_key_ref, q_at, k_at), (w_value_ref, k_at, k_at + kv_width))
        return [
            pltpu.make_async_copy(
                ref.at[0, cols(n), :], wqkv.at[n, :, pl.ds(lo, hi - lo)], w_sem.at[n, i]
            )
            for i, (ref, lo, hi) in enumerate(pieces)
        ]

    def wo_copy(n):
        return pltpu.make_async_copy(w_out_ref.at[0, :, cols(n)], wout.at[n], wo_sem.at[n])

    def e_copy(m, n):
        return pltpu.make_async_copy(embeds_ref.at[m, :, cols(n)], full.at[m, n, t], e_sem.at[m, n])

    head_copy = pltpu.make_async_copy(head_ref, whead, wh_sem)

    @pl.when(p == 0)
    def _():
        for m in range(micro):
            for n in range(n_chunk):
                e_copy(m, n).start()

    for n in range(n_chunk):
        for copy in w_copies(n):
            copy.start()

    @pl.when(p > 0)
    def _():
        for n in range(n_chunk):
            wo_copy(n).start()
        head_copy.start()

    def ring(j):
        peer = lax.rem(slot + j, group)
        return peer, {"pipe": peer // n_tensor, "tensor": lax.rem(peer, n_tensor)}

    barrier = pltpu.get_barrier_semaphore()
    for j in range(1, group):
        pl.semaphore_signal(barrier, inc=1, device_id=ring(j)[1], device_id_type=MESH)
    pl.semaphore_wait(barrier, group - 1)

    def remote(src, dst, send, recv, device):
        return pltpu.make_async_remote_copy(
            src_ref=src, dst_ref=dst, send_sem=send, recv_sem=recv,
            device_id=device, device_id_type=MESH,
        )

    def mate(j):
        return lax.rem(t + j, n_tensor)

    def in_copy(m, n):
        return remote(outst.at[m, n], full.at[m, n, t], in_send.at[m, n], in_recv.at[m, n],
                      {"pipe": lax.rem(p + 1, n_pipe)})

    def g_copy(m, n, j):
        return remote(full.at[m, n, t], full.at[m, n, t], g_send.at[m, n, j], g_recv.at[m, n, t],
                      {"tensor": mate(j)})

    def g_arrival(m, n, j):
        who = mate(j)
        return remote(full.at[m, n, who], full.at[m, n, who], g_send.at[m, n, j],
                      g_recv.at[m, n, who], {"tensor": who})

    def r_copy(m, n, j):
        who = mate(j)
        return remote(part.at[m, n, who], rs.at[m, n, t], r_send.at[m, n, j],
                      r_recv.at[m, n, t], {"tensor": who})

    def r_arrival(m, n, j):
        who = mate(j)
        return remote(part.at[m, n, who], rs.at[m, n, who], r_send.at[m, n, j],
                      r_recv.at[m, n, who], {"tensor": who})

    def h_copy(m, n, k, to):
        piece = fin.at[m, n, t]
        return remote(piece, piece, h_send.at[m, n, k], h_recv.at[m, n], {"pipe": to})

    def s_copy(m, n, j):
        return remote(fin.at[m, n, t], fin.at[m, n, t], s_send.at[m, n, j], s_recv.at[m, n, t],
                      {"tensor": mate(j)})

    def s_arrival(m, n, j):
        who = mate(j)
        return remote(fin.at[m, n, who], fin.at[m, n, who], s_send.at[m, n, j],
                      s_recv.at[m, n, who], {"tensor": who})

    def scaled(squares):
        return lax.rsqrt(squares * (1.0 / width) + EPSILON)

    row_at = lax.broadcasted_iota(jnp.int32, (per_kv * seq_len, seq_len), 0)
    key_at = lax.broadcasted_iota(jnp.int32, (per_kv * seq_len, seq_len), 1)
    causal = lax.rem(row_at, seq_len) >= key_at
    no_squares = jnp.zeros((step_len, 1), jnp.float32)

    def layer(m, carry):
        def arrive(n):
            @pl.when(p > 0)
            def _():
                in_copy(m, n).wait_recv()

            @pl.when(p == 0)
            def _():
                e_copy(m, n).wait()

            for j in range(1, n_tensor):
                g_copy(m, n, j).start()

        acc[...] = jnp.zeros_like(acc)
        for n in range(lag_in):
            arrive(n)

        def project(n, squares):
            @pl.when(n + lag_in < n_chunk)
            def _():
                arrive(n + lag_in)

            for j in range(1, n_tensor):
                g_arrival(m, n, j).wait_recv()

            @pl.when(m == 0)
            def _():
                for copy in w_copies(n):
                    copy.wait()

            @pl.when((m == 0) & (p == 0) & (n == n_chunk - 2))
            def _():
                for i in range(n_chunk):
                    wo_copy(i).start()

            wide = full[m, n].astype(jnp.float32).reshape(step_len, chunk)
            lhs = (wide * gain_ref[:, cols(n)]).astype(jnp.bfloat16)
            for at in range(0, q_width + 2 * kv_width, kv_width):
                acc[:, at : at + kv_width] += jnp.dot(
                    lhs, wqkv[n, :, at : at + kv_width], preferred_element_type=jnp.float32
                )
            return squares + jnp.sum(wide * wide, axis=-1, keepdims=True)

        factor = scaled(lax.fori_loop(0, n_chunk, project, no_squares))

        @pl.when((m == 0) & (p == 0))
        def _():
            head_copy.start()

        def of_sequence(value, b):
            starts = [i * rows + b * own_rows for i in range(n_tensor)]
            return jnp.concatenate([value[at : at + own_rows] for at in starts], axis=0)

        def attend(b):
            own_factor = of_sequence(factor, b)
            cosine, sine = cos_ref[...] * own_factor, sin_ref[...] * own_factor

            def head_of(at):
                starts = [i * rows + b * own_rows for i in range(n_tensor)]
                return jnp.concatenate(
                    [acc[lo : lo + own_rows, at : at + HD] for lo in starts], axis=0
                )

            def turned(at):
                one = head_of(at)
                return (one * cosine + pltpu.roll(one, HD // 2, 1) * sine).astype(jnp.bfloat16)

            for h in range(heads_kv):
                queries = [turned((h * per_kv + g) * HD) for g in range(per_kv)]
                query = jnp.concatenate(queries, axis=0) if per_kv > 1 else queries[0]
                key = turned(q_width + h * HD)
                value = (head_of(q_width + kv_width + h * HD) * own_factor).astype(jnp.bfloat16)
                scores = lax.dot_general(
                    query, key, (((1,), (1,)), ((), ())), preferred_element_type=jnp.float32
                ) * (1.0 / math.sqrt(HD))
                scores = jnp.where(causal, scores, NEG)
                shifted = jnp.exp(scores - jnp.max(scores, axis=-1, keepdims=True))
                probs = (shifted / jnp.sum(shifted, axis=-1, keepdims=True)).astype(jnp.bfloat16)
                context = jnp.dot(probs, value, preferred_element_type=jnp.float32)
                for g in range(per_kv):
                    at = (h * per_kv + g) * HD
                    for i in range(n_tensor):
                        lo, frm = i * rows + b * own_rows, g * seq_len + i * own_rows
                        ctx[lo : lo + own_rows, at : at + HD] = context[
                            frm : frm + own_rows
                        ].astype(jnp.bfloat16)

        for b in range(batch):
            attend(b)

        def combine(n):
            block = part[m, n, t].astype(jnp.float32)
            for j in range(1, n_tensor):
                r_arrival(m, n, j).wait_recv()
                block += rs[m, n, mate(j)].astype(jnp.float32)
            state = (full[m, n, t].astype(jnp.float32) + block).astype(jnp.bfloat16)

            @pl.when(p < last)
            def _():
                outst[m, n] = state
                in_copy(m, n).start()

            @pl.when(p == last)
            def _():
                fin[m, n, t] = state
                for k, to in enumerate(near):
                    h_copy(m, n, k, to).start()

        def output(n, c):
            @pl.when(m == 0)
            def _():
                wo_copy(n).wait()

            product = jnp.dot(ctx[...], wout[n], preferred_element_type=jnp.float32)
            part[m, n] = product.reshape(n_tensor, rows, chunk).astype(jnp.bfloat16)
            for j in range(1, n_tensor):
                r_copy(m, n, j).start()

            @pl.when(n >= lag_out)
            def _():
                combine(n - lag_out)

            return c

        lax.fori_loop(0, n_chunk, output, 0)
        for n in range(n_chunk - lag_out, n_chunk):
            combine(n)
        return carry

    lax.fori_loop(0, micro, layer, 0)

    lab_pad = jnp.zeros((LANES - micro * batch, seq_len), jnp.float32)
    lab = jnp.concatenate([labels_ref[...].astype(jnp.float32), lab_pad], axis=0).T
    few = lax.broadcasted_iota(jnp.int32, (own_rows, LANES), 1)
    for i in range(n_tensor):
        for b in range(batch):
            block = jnp.zeros((own_rows, LANES), jnp.float32)
            for m in range(micro):
                at = m * batch + b
                column = lab[i * own_rows : (i + 1) * own_rows, at : at + 1]
                block = jnp.where(few == m, column, block)
            lo = i * rows + b * own_rows
            labcol[lo : lo + own_rows, :] = block
    slab[...] = jnp.zeros_like(slab)
    lane = lax.broadcasted_iota(jnp.int32, (step_len, LANES), 1)
    entry = (lax.broadcasted_iota(jnp.int32, (step_len, vocab_dev), 1) + slot * vocab_dev).astype(
        jnp.float32
    )
    head_copy.wait()

    def head(m, carry):
        def arrive(n):
            @pl.when(p < last)
            def _():
                h_copy(m, n, 0, last).wait_recv()

            if far:
                for k in range(2):
                    @pl.when((p == near[k]) & (lax.rem(n, 2) == k))
                    def _():
                        for f, to in enumerate(far):
                            h_copy(m, n, f, to).start()

            for j in range(1, n_tensor):
                s_copy(m, n, j).start()

        logits[m] = jnp.zeros_like(logits[m])
        ghid[m] = jnp.zeros_like(ghid[m])
        for n in range(lag_in):
            arrive(n)

        def score(n, squares):
            @pl.when(n + lag_in < n_chunk)
            def _():
                arrive(n + lag_in)

            for j in range(1, n_tensor):
                s_arrival(m, n, j).wait_recv()
            wide = fin[m, n].astype(jnp.float32).reshape(step_len, chunk)
            lhs = (wide * final_gain_ref[:, cols(n)]).astype(jnp.bfloat16)
            logits[m] += jnp.dot(lhs, whead[cols(n), :], preferred_element_type=jnp.float32)
            ghid[m] += lax.dot_general(
                lhs, lhs, (((1,), (1,)), ((), ())), preferred_element_type=jnp.float32
            )
            return squares + jnp.sum(wide * wide, axis=-1, keepdims=True)

        factor = scaled(lax.fori_loop(0, n_chunk, score, no_squares))
        local = logits[m] * factor
        logits[m] = local
        own = jnp.sum(jnp.where(lane == m, labcol[...], 0.0), axis=-1, keepdims=True)
        peak = jnp.max(local, axis=-1, keepdims=True)
        mass = jnp.sum(jnp.exp(local - peak), axis=-1, keepdims=True)
        target = jnp.sum(jnp.where(entry == own, local, 0.0), axis=-1, keepdims=True)
        kept = slab[...]
        for i, column in enumerate((peak, mass, target, factor)):
            kept = jnp.where(lane == i * micro + m, column, kept)
        slab[...] = kept
        return carry

    lax.fori_loop(0, micro, head, 0)

    n_stats = stats.shape[1]
    slab_cols = slab[...]
    stats[slot] = slab_cols.T[:n_stats]

    def exchange(buffer, send, recv):
        def copy(j):
            peer, device = ring(j)
            return remote(buffer.at[slot], buffer.at[slot], send.at[j], recv.at[slot], device)

        def arrival(j):
            peer, device = ring(j)
            return remote(buffer.at[peer], buffer.at[peer], send.at[j], recv.at[peer], device)

        for j in range(1, group):
            copy(j).start()
        for j in range(1, group):
            arrival(j).wait_recv()
        return copy

    stats_copy = exchange(stats, t_send, t_recv)
    peaks = stats[:, :micro, :]
    peak_row = jnp.max(peaks, axis=0)
    masses = jnp.exp(peaks - peak_row[None]) * stats[:, micro : 2 * micro, :]
    log_norm = peak_row + jnp.log(jnp.sum(masses, axis=0))
    loss_ref[...] = log_norm - jnp.sum(stats[:, 2 * micro : 3 * micro, :], axis=0)
    factor_rows = stats[0, 3 * micro : 4 * micro, :]
    labels_t = labcol[...]
    pad = jnp.zeros((LANES - micro, step_len), jnp.float32)
    norm_t = jnp.concatenate([log_norm, pad], axis=0).T

    def sequence_at(shape, dim):
        return lax.rem(lax.div(lax.broadcasted_iota(jnp.int32, shape, dim), own_rows), batch)

    square = (step_len, step_len)
    same = sequence_at(square, 0) == sequence_at(square, 1)

    tot_rows = tots.shape[1]
    row_id = lax.broadcasted_iota(jnp.int32, (tot_rows, step_len), 0)
    sums = jnp.zeros((tot_rows, step_len), jnp.float32)
    for m in range(micro):
        onehot = (entry == labels_t[:, m : m + 1]).astype(jnp.float32)
        errors = (jnp.exp(logits[m] - norm_t[:, m : m + 1]) - onehot).astype(jnp.bfloat16)
        gram = lax.dot_general(
            errors, errors, (((1,), (1,)), ((), ())), preferred_element_type=jnp.float32
        )
        f_at = 3 * micro + m
        weighted = jnp.where(same, gram * ghid[m] * slab_cols[:, f_at : f_at + 1], 0.0)
        row = jnp.sum(weighted, axis=0, keepdims=True) * factor_rows[m : m + 1]
        sums = jnp.where(row_id == m, row, sums)
    tots[slot] = sums
    tots_copy = exchange(tots, u_send, u_recv)
    total = jnp.sum(tots[...], axis=0)
    of_row = sequence_at((tot_rows, step_len), 1)
    out_lane = lax.broadcasted_iota(jnp.int32, score_ref.shape, 1)
    scored = jnp.zeros(score_ref.shape, jnp.float32)
    for b in range(batch):
        own = jnp.sum(jnp.where(of_row == b, total, 0.0), axis=-1, keepdims=True)
        scored = jnp.where(out_lane == b, jnp.sqrt(own) / seq_len, scored)
    score_ref[...] = scored

    def drain(m, carry):
        for n in range(n_chunk):
            for j in range(1, n_tensor):
                g_copy(m, n, j).wait_send()
                s_copy(m, n, j).wait_send()
                r_copy(m, n, j).wait_send()

        @pl.when(p < last)
        def _():
            for n in range(n_chunk):
                in_copy(m, n).wait_send()

        @pl.when(p == last)
        def _():
            for n in range(n_chunk):
                for k, to in enumerate(near):
                    h_copy(m, n, k, to).wait_send()

        if far:
            for k in range(2):
                @pl.when(p == near[k])
                def _():
                    for n in range(k, n_chunk, 2):
                        for f, to in enumerate(far):
                            h_copy(m, n, f, to).wait_send()

        return carry

    lax.fori_loop(0, micro, drain, 0)
    for j in range(1, group):
        stats_copy(j).wait_send()
        tots_copy(j).wait_send()


def per_device(embeds, labels, norm_gain, w_query, w_key, w_value, w_out, final_gain, head_weight):
    n_pipe = lax.axis_size("pipe")
    n_tensor = lax.axis_size("tensor")
    group = n_pipe * n_tensor
    sequences, own_rows, width = embeds.shape
    seq_len = own_rows * n_tensor
    batch = 1
    micro, rows = sequences // batch, batch * own_rows
    step_len = rows * n_tensor
    heads_q = w_query.shape[2] // HD
    heads_kv = w_key.shape[2] // HD
    qkv_width = (heads_q + 2 * heads_kv) * HD
    depth = w_out.shape[1]
    vocab_dev = head_weight.shape[1]
    n_chunk, lag_in, lag_out = 8, 2, 2
    chunk = width // n_chunk
    n_far = max(n_pipe, 2)
    cos_table, sin_table = rotary_tables(seq_len)
    dims = (n_pipe, n_tensor, micro, batch, own_rows, width, heads_q, heads_kv, vocab_dev, lag_in, lag_out)
    bf16, f32 = jnp.bfloat16, jnp.float32
    dma = pltpu.SemaphoreType.DMA
    any_spec = pl.BlockSpec(memory_space=pl.ANY)
    vmem_spec = pl.BlockSpec(memory_space=pltpu.VMEM)
    stat_rows = round_up(4 * micro, 8)
    tot_rows = round_up(micro, 8)
    losses, scores = pl.pallas_call(
        functools.partial(relay_kernel, dims),
        out_shape=(
            jax.ShapeDtypeStruct((micro, step_len), f32),
            jax.ShapeDtypeStruct((tot_rows, LANES), f32),
        ),
        in_specs=[any_spec, vmem_spec, vmem_spec] + [any_spec] * 4
        + [vmem_spec, any_spec, vmem_spec, vmem_spec],
        out_specs=(vmem_spec, vmem_spec),
        scratch_shapes=[
            pltpu.VMEM((n_chunk, chunk, qkv_width), bf16),
            pltpu.VMEM((n_chunk, depth, chunk), bf16),
            pltpu.VMEM((width, vocab_dev), bf16),
            pltpu.VMEM((micro, n_chunk, n_tensor, rows, chunk), bf16),
            pltpu.VMEM((step_len, qkv_width), f32),
            pltpu.VMEM((step_len, depth), bf16),
            pltpu.VMEM((micro, n_chunk, n_tensor, rows, chunk), bf16),
            pltpu.VMEM((micro, n_chunk, n_tensor, rows, chunk), bf16),
            pltpu.VMEM((micro, n_chunk, rows, chunk), bf16),
            pltpu.VMEM((micro, n_chunk, n_tensor, rows, chunk), bf16),
            pltpu.VMEM((micro, step_len, vocab_dev), f32),
            pltpu.VMEM((micro, step_len, step_len), f32),
            pltpu.VMEM((step_len, LANES), f32),
            pltpu.VMEM((step_len, LANES), f32),
            pltpu.VMEM((group, stat_rows, step_len), f32),
            pltpu.VMEM((group, tot_rows, step_len), f32),
            dma((n_chunk, 3)), dma((n_chunk,)), dma, dma((micro, n_chunk)),
            dma((micro, n_chunk)), dma((micro, n_chunk)),
            dma((micro, n_chunk, n_tensor)), dma((micro, n_chunk, n_tensor)),
            dma((micro, n_chunk, n_tensor)), dma((micro, n_chunk, n_tensor)),
            dma((micro, n_chunk, n_far)), dma((micro, n_chunk)),
            dma((micro, n_chunk, n_tensor)), dma((micro, n_chunk, n_tensor)),
            dma((group,)), dma((group,)), dma((group,)), dma((group,)),
        ],
        compiler_params=pltpu.CompilerParams(
            collective_id=0, has_side_effects=True, vmem_limit_bytes=58 * 1024 * 1024
        ),
    )(
        embeds.reshape(micro, rows, width), labels, norm_gain, w_query, w_key, w_value, w_out,
        final_gain.reshape(1, width), head_weight, jnp.asarray(cos_table), jnp.asarray(sin_table),
    )
    loss_width = seq_len // group
    device_slot = lax.axis_index("pipe") * n_tensor + lax.axis_index("tensor")
    losses = losses.reshape(micro, n_tensor, batch, own_rows).transpose(0, 2, 1, 3)
    losses = losses.reshape(sequences, seq_len)
    token_loss = lax.dynamic_slice_in_dim(losses, device_slot * loss_width, loss_width, 1)
    return (token_loss, scores[:micro, :batch].reshape(sequences))


def solution(mesh):
    in_specs = (
        P("dp", "tensor", None),
        P("dp", None),
        P("pipe", None),
        P("pipe", None, "tensor"),
        P("pipe", None, "tensor"),
        P("pipe", None, "tensor"),
        P("pipe", "tensor", None),
        P(),
        P(None, ("pipe", "tensor")),
    )
    out_specs = (P("dp", ("pipe", "tensor")), P("dp"))
    return jax.shard_map(
        per_device, mesh=mesh, in_specs=in_specs, out_specs=out_specs, check_vma=False
    )
```
